32 devices in a mesh: seq: 8 (over y, x, core), batch: 4 (over z).
Axes of the slice: x: 2, y: 2, z: 4, core: 2. Of those that a mesh axis runs over, the one named last changes fastest.
Arguments:
- ssm_input: bfloat16 [8192, 4096], P(('batch', 'seq')), parts along dimension 0, may hold values from -6 to 6
- gate_input: bfloat16 [8192, 4096], P(('batch', 'seq')), parts along dimension 0, may hold values from -6 to 6
- b_rows: bfloat16 [8192, 128], P(('batch', 'seq')), parts along dimension 0, may hold values from -6 to 6
- c_rows: bfloat16 [8192, 128], P(('batch', 'seq')), parts along dimension 0, may hold values from -6 to 6
- step_raw: float32 [8192, 64], P(('batch', 'seq')), parts along dimension 0, may hold values from -14 to 2
- step_bias: float32 [64], replicated, may hold values from -0.5 to 0.5
- rate_log: float32 [64], replicated, may hold values from -1.5 to 4
- skip_gain: float32 [64], replicated, may hold values from 0.5 to 2
- norm_gain: float32 [4096], replicated, may hold values from 0.5 to 1.5
- w_out: bfloat16 [4096, 4096], P(None, 'seq'), may hold values from -0.09375 to 0.09375
- residual: bfloat16 [8192, 4096], P(('batch', 'seq')), parts along dimension 0, may hold values from -6 to 6
- moe_gain: float32 [4096], replicated, may hold values from 0.5 to 1.5
- router: bfloat16 [4096, 8], replicated, may hold values from -0.09375 to 0.09375
- expert_ids: int32 [8192, 2], P(('batch', 'seq')), parts along dimension 0, may hold values from 0 to 7, all different within a row; in each aligned block of 256 rows (0 to 255, 256 to 511, ...) at most 96 rows name the same one
- w_gate: bfloat16 [8, 4096, 384], P('seq'), may hold values from -0.09375 to 0.09375
- w_up: bfloat16 [8, 4096, 384], P('seq'), may hold values from -0.09375 to 0.09375
- w_down: bfloat16 [8, 384, 4096], P('seq'), may hold values from -0.3125 to 0.3125
Outputs:
- layer_out: bfloat16 [8192, 4096], P(('batch', 'seq')), parts along dimension 0
The draws below stay inside these ranges and needn't reach their ends.
There are 4 independent parts, one for each index of `batch`. The reference program is written for one: setup_inputs(seed, part) draws one part's arguments, and reference() takes and returns one part's arrays. A program takes and returns all parts, laid end to end along the dimension named above; an argument that names none is the same for every part. Nothing has to cross between parts.
Inputs may be any that keep to these rules, and one draw needn't show every extreme that they name: `expert_ids`: the 2 ids of a token differ. In the rows of one device (256 rows, aligned blocks), no expert is named by more than 96 rows, a bound that some block reaches.
All inputs are finite; a program needn't handle non-finite values.
Results may differ from the reference program's by a relative error of at most 0.008.
Values may be sent and summed in bfloat16 or wider, within the bound.
A program may use at most 192 MiB of HBM per device.

```python
import math
import jax
import jax.numpy as jnp
import numpy as np
from jax import lax

D = 4096
HEADS = 64
HEAD_DIM = 64
STATE = 128
D_IN = 4096
FF = 384
TOP = 2
GROUP = 256
TOK_DEV = 256
LEN = 2048
EXPERTS = 8
CAP = 96
N_SEQ = 8


def draw_rate_log(key, part):
    first, second, third = jax.random.split(key, 3)
    fast = jax.random.bernoulli(first, 0.5, (HEADS,))
    slow_rate = jnp.exp(jax.random.uniform(second, (HEADS,), jnp.float32, math.log(0.25), math.log(0.45)))
    fast_rate = LEN / 3.0 * jnp.exp(jax.random.uniform(third, (HEADS,), jnp.float32, math.log(1.0 / 50.0), math.log(1.0 / 30.0)))
    chosen = jnp.log(jnp.where(fast, fast_rate, slow_rate))
    return jnp.minimum(chosen, 4.0).astype(jnp.float32)


def draw_step_raw(key, part):
    first, second, third, fourth = jax.random.split(key, 4)
    noise = 0.4 * jax.random.normal(first, (LEN, HEADS), jnp.float32)
    slabs = jax.random.uniform(second, (LEN // TOK_DEV, HEADS), jnp.float32, -0.6, 0.6)
    slab_shift = jnp.repeat(slabs, TOK_DEV, axis=0)
    starting_offset = math.log(3.0 / LEN) + noise + slab_shift
    expert_slot_positions = jax.random.randint(third, (2,), 0, LEN)
    position_indices = jnp.arange(LEN)
    token_group_size = jnp.any(position_indices[:, None] == expert_slot_positions[None, :], axis=1)
    doubling_depth = jax.random.uniform(fourth, (LEN, HEADS), jnp.float32, 0.0, 1.1)
    return jnp.where(token_group_size[:, None], doubling_depth, starting_offset).astype(jnp.float32)


def block_levels(stream_key, dims, cuts, low, top_value):
    level, own = 1.0, jax.random.fold_in(stream_key, 6)
    for axis_at, parts in cuts:
        draws = jnp.exp(jax.random.uniform(jax.random.fold_in(own, axis_at), (parts,), jnp.float32, low / len(cuts), top_value / len(cuts)))
        level = level * jnp.repeat(draws, dims[axis_at] // parts).reshape([-1 if axis == axis_at else 1 for axis in range(len(dims))])
    return level


def shared_out(stream_key, own, number, rows, amount, top, bound, skew):
    ranking = jax.random.permutation(stream_key, amount)
    heavy_load, usual = load_shares(amount, rows * top, bound, skew, True), load_shares(amount, rows * top, bound, skew, False)
    places = jnp.arange(amount)

    def named(sizes, offset_by):
        used = int((sizes > 0).sum())
        fixed = max(1, used // 4)
        moved = fixed + (places - fixed + offset_by * (used - fixed)) % max(1, amount - fixed)
        return jnp.zeros((amount,), jnp.int32).at[ranking[jnp.where(places < fixed, places, moved)]].set(jnp.asarray(sizes, jnp.int32))

    sizes = jnp.where(number % 4 == 0, named(heavy_load, number // 4), named(usual, number - number // 4 - 1))
    mixed = jax.random.permutation(jax.random.fold_in(own, 3), amount)
    donor, taker = mixed[0:amount // 2 * 2:2], mixed[1:amount // 2 * 2:2]
    room = jnp.minimum(sizes[donor] - 1, bound - sizes[taker]) // 2
    room = jnp.where((donor == ranking[0]) | (taker == ranking[0]) | (sizes[taker] == 0), 0, jnp.maximum(room, 0))
    moved = jax.random.randint(jax.random.fold_in(own, 4), (amount // 2,), 0, 1 << 20) % (room + 1)
    sizes = sizes.at[donor].add(-moved).at[taker].add(moved)
    labels = jnp.searchsorted(jnp.cumsum(sizes), jnp.arange(rows * top), side="right").astype(jnp.int32)
    listing = labels.reshape(top, rows).T
    listing = listing[jax.random.permutation(jax.random.fold_in(own, 1), rows)]
    offset_by = jax.random.randint(jax.random.fold_in(own, 2), (rows, 1), 0, top)
    return jnp.take_along_axis(listing, (jnp.arange(top)[None, :] + offset_by) % top, axis=1)


def load_shares(amount, total, most, skew, full):
    weights = [(1 << 20) // math.isqrt(standing ** skew) + 1 for standing in range(1, amount + 1)]
    largest = most if full else min(most, max(-(-total // amount), total * weights[0] // sum(weights)))
    least = 1 if total - largest >= amount - 1 else 0
    holding, rest = [largest] + [least] * (amount - 1), total - largest - least * (amount - 1)
    while rest > 0:
        free = [i for i in range(1, amount) if holding[i] < largest] or [i for i in range(1, amount) if holding[i] < most]
        pool, budget = sum([weights[i] for i in free]), rest
        for i in free:
            extra = min(most - holding[i], max(1, budget * weights[i] // pool), rest)
            holding[i] = holding[i] + extra
            rest = rest - extra
    return np.array(holding)


def gaussian(rng, shape, scale, reach, shards=(), dtype=jnp.bfloat16):
    values = jax.random.normal(rng, shape, jnp.float32) * scale
    if len(shards) > 0:
        values = block_levels(rng, shape, shards, -0.22, 0.18) * values
    return jnp.clip(values, min=-reach, max=reach).astype(dtype)


def setup_inputs(seed: int = 0, part: int = 0) -> dict:
    seeds = jax.random.split(jax.random.key(seed), 18)
    part_splits = jax.random.split(jax.random.fold_in(seeds[17], part), 18)
    ssm_input = gaussian(part_splits[0], (LEN, D_IN), 1.0, 6.0, ((0, 8),))
    gate_input = gaussian(part_splits[1], (LEN, D_IN), 1.0, 6.0, ((0, 8),))
    b_rows = gaussian(part_splits[2], (LEN, STATE), 1.0, 6.0, ((0, 8),))
    c_rows = gaussian(part_splits[3], (LEN, STATE), 1.0, 6.0, ((0, 8),))
    step_raw = draw_step_raw(jax.random.fold_in(jax.random.fold_in(seeds[17], part), 71), part)
    step_bias = jnp.clip(jax.random.uniform(seeds[5], (HEADS,), jnp.float32, -0.5, 0.5), -0.5, 0.5)
    rate_log = draw_rate_log(jax.random.fold_in(seeds[17], 71), part)
    skip_gain = jnp.clip(jax.random.uniform(seeds[7], (HEADS,), jnp.float32, 0.5, 2.0), 0.5, 2.0)
    norm_gain = jnp.clip(1.0 + 0.1 * jax.random.normal(seeds[8], (D_IN,), jnp.float32), 0.5, 1.5)
    w_out = gaussian(seeds[9], (D_IN, D), D_IN ** -0.5, 0.09375, ((1, 8),))
    residual = gaussian(part_splits[10], (LEN, D), 1.0, 6.0, ((0, 8),))
    moe_gain = jnp.clip(1.0 + 0.1 * jax.random.normal(seeds[11], (D,), jnp.float32), 0.5, 1.5)
    router = gaussian(seeds[12], (D, EXPERTS), D ** -0.5, 0.09375)
    expert_ids_keys = jax.random.split(jax.random.fold_in(part_splits[13], 1), LEN // TOK_DEV)
    expert_ids_turns = jax.random.permutation(jax.random.fold_in(part_splits[13], 3), LEN // TOK_DEV)
    expert_ids = jax.vmap(lambda own, number: shared_out(jax.random.fold_in(part_splits[13], 2), own, number, TOK_DEV, EXPERTS, TOP, CAP, 1))(expert_ids_keys, expert_ids_turns).reshape((LEN, TOP))
    w_gate = gaussian(seeds[14], (EXPERTS, D, FF), D ** -0.5, 0.09375, ((0, 8),))
    w_up = gaussian(seeds[15], (EXPERTS, D, FF), D ** -0.5, 0.09375, ((0, 8),))
    w_down = gaussian(seeds[16], (EXPERTS, FF, D), FF ** -0.5, 0.3125, ((0, 8),))
    return dict(ssm_input=ssm_input, gate_input=gate_input, b_rows=b_rows, c_rows=c_rows, step_raw=step_raw, step_bias=step_bias, rate_log=rate_log, skip_gain=skip_gain, norm_gain=norm_gain, w_out=w_out, residual=residual, moe_gain=moe_gain, router=router, expert_ids=expert_ids, w_gate=w_gate, w_up=w_up, w_down=w_down)


def group_pass(carried, pieces):
    inputs, b_block, c_block, steps_h, logs_h = pieces
    running = jnp.cumsum(logs_h, axis=0)
    length = logs_h.shape[0]
    scores = jnp.dot(c_block, b_block.T, preferred_element_type=jnp.float32)
    causal = jnp.arange(length)[:, None] >= jnp.arange(length)[None, :]
    spread = running[:, None, :] - running[None, :, :]
    decays = jnp.exp(jnp.where(causal[:, :, None], spread, -jnp.inf))
    mixing = (scores[:, :, None] * decays * steps_h[None, :, :]).astype(jnp.bfloat16)
    inputs32 = inputs.astype(jnp.float32)
    intra = jnp.einsum('tsh,shp->thp', mixing.astype(jnp.float32), inputs32, precision=lax.Precision.HIGHEST)
    c_wide = c_block.astype(jnp.float32)
    from_state = jnp.exp(running)[:, :, None] * jnp.einsum('tn,hpn->thp', c_wide, carried, precision=lax.Precision.HIGHEST)
    departing_state = jnp.exp(running[-1][None, :] - running) * steps_h
    block_in = (departing_state[:, :, None] * b_block.astype(jnp.float32)[:, None, :]).astype(jnp.bfloat16)
    update = jnp.einsum('shn,shp->hpn', block_in.astype(jnp.float32), inputs32, precision=lax.Precision.HIGHEST)
    new_carried = jnp.exp(running[-1])[:, None, None] * carried + update
    return (new_carried, intra + from_state)

def reference(ssm_input, gate_input, b_rows, c_rows, step_raw, step_bias, rate_log, skip_gain, norm_gain, w_out, residual, moe_gain, router, expert_ids, w_gate, w_up, w_down):
    blocks = LEN // GROUP
    step_sizes = jax.nn.softplus(step_raw + step_bias[None, :])
    log_decay = -step_sizes * jnp.exp(rate_log)[None, :]
    inputs = ssm_input.reshape(blocks, GROUP, HEADS, HEAD_DIM)
    pieces = (inputs, b_rows.reshape(blocks, GROUP, STATE), c_rows.reshape(blocks, GROUP, STATE), step_sizes.reshape(blocks, GROUP, HEADS), log_decay.reshape(blocks, GROUP, HEADS))
    start = jnp.zeros((HEADS, HEAD_DIM, STATE), jnp.float32)
    final_state, outputs = lax.scan(group_pass, start, pieces)
    ssm_out = outputs.reshape(LEN, HEADS, HEAD_DIM) + skip_gain[None, :, None] * ssm_input.reshape(LEN, HEADS, HEAD_DIM).astype(jnp.float32)
    gated = ssm_out.reshape(LEN, D_IN) * jax.nn.silu(gate_input.astype(jnp.float32))
    normed = (gated * lax.rsqrt(lax.optimization_barrier(jnp.mean(gated * gated, axis=1, keepdims=True)) + 1e-05) * norm_gain[None, :]).astype(jnp.bfloat16)
    mixer_out = jnp.dot(normed, w_out, preferred_element_type=jnp.float32).astype(jnp.bfloat16)
    hidden = (residual.astype(jnp.float32) + mixer_out.astype(jnp.float32)).astype(jnp.bfloat16)
    hidden_wide = hidden.astype(jnp.float32)
    moe_input = (hidden_wide * lax.rsqrt(lax.optimization_barrier(jnp.mean(hidden_wide * hidden_wide, axis=1, keepdims=True)) + 1e-05) * moe_gain[None, :]).astype(jnp.bfloat16)
    logits = jnp.dot(moe_input, router, preferred_element_type=jnp.float32)
    chosen = jnp.take_along_axis(logits, expert_ids, axis=1)
    powers = jnp.exp(chosen)
    combine = powers / lax.optimization_barrier(jnp.sum(powers, axis=1, keepdims=True))
    flat_ids = expert_ids.reshape(-1)
    flat_combine = combine.reshape(-1)
    capacity = N_SEQ * CAP
    total = hidden_wide
    for expert in range(EXPERTS):
        picked = flat_ids == expert
        count = jnp.sum(picked.astype(jnp.int32))
        rows = jnp.nonzero(picked, size=capacity, fill_value=0)[0].astype(jnp.int32)
        valid = (jnp.arange(capacity) < count).astype(jnp.float32)
        token_of = (rows // TOP).astype(jnp.int32)
        taken = moe_input[token_of]
        gate_part = jnp.dot(taken, w_gate[expert], preferred_element_type=jnp.float32)
        up_part = jnp.dot(taken, w_up[expert], preferred_element_type=jnp.float32)
        expert_hidden = (jax.nn.silu(gate_part) * up_part).astype(jnp.bfloat16)
        expert_out = jnp.dot(expert_hidden, w_down[expert], preferred_element_type=jnp.float32).astype(jnp.bfloat16)
        scaled = expert_out.astype(jnp.float32) * (flat_combine[rows] * valid)[:, None]
        total = total.at[token_of].add(scaled)
    return total.astype(jnp.bfloat16)
```

```python
import jax
import jax.numpy as jnp
from jax import lax
from jax.sharding import PartitionSpec as P

GROUP = 256
LOW = 4
HIGHEST = lax.Precision.HIGHEST
F32 = jnp.float32
BF16 = jnp.bfloat16


def three_parts(x):
    first = lax.reduce_precision(x, 8, 7)
    rest = x - first
    second = lax.reduce_precision(rest, 8, 7)
    return first, second, rest - second


def shards(
    ssm_input,
    gate_input,
    b_rows,
    c_rows,
    step_raw,
    step_bias,
    rate_log,
    skip_gain,
    norm_gain,
    w_out,
    residual,
    moe_gain,
    router,
    expert_ids,
    w_gate,
    w_up,
    w_down,
):
    n = lax.axis_size("seq")
    tokens = ssm_input.shape[0]
    inner = ssm_input.shape[1]
    heads = rate_log.shape[0]
    head_width = inner // heads
    state_width = b_rows.shape[1]
    assert tokens == GROUP
    high = n // LOW

    groups = [[a * LOW + b for b in range(LOW)] for a in range(high)]
    w_group = lax.all_gather(w_out, "seq", axis=0, axis_index_groups=groups)

    at = jnp.arange(tokens)
    causal = at[:, None] >= at[None, :]
    step_sizes = jax.nn.softplus(step_raw + step_bias[None, :])
    log_decay = -step_sizes * jnp.exp(rate_log)[None, :]
    running = jnp.dot(causal.astype(F32), log_decay, precision=HIGHEST)
    total = running[-1]
    inputs = ssm_input.reshape(tokens, heads, head_width)

    departing = jnp.exp(total[None, :] - running) * step_sizes
    block_in = (departing[:, :, None] * b_rows.astype(F32)[:, None, :]).astype(BF16)
    update = jnp.einsum("shn,shp->hpn", block_in, inputs, preferred_element_type=F32)
    first, second, third = three_parts(total)
    row = jnp.arange(16)[None, :]
    extra = jnp.where(
        row == 0,
        first[:, None],
        jnp.where(row == 1, second[:, None], jnp.where(row == 2, third[:, None], 0.0)),
    )
    extra = jnp.broadcast_to(extra[:, :, None], (heads, 16, state_width))
    packet = jnp.concatenate([update.astype(BF16), extra.astype(BF16)], axis=1)
    share = heads // n
    packet = packet.reshape(n, share, head_width + 16, state_width)
    packet = lax.all_to_all(packet, "seq", split_axis=0, concat_axis=0, tiled=True)
    logs = jnp.sum(packet[:, :, head_width : head_width + 3, 0].astype(F32), axis=2)
    decays = jnp.exp(logs)
    carried = jnp.zeros((share, head_width, state_width), F32)
    entering = []
    for k in range(n):
        entering.append(carried.astype(BF16))
        carried = decays[k][:, None, None] * carried + packet[k, :, :head_width].astype(F32)
    entering = jnp.stack(entering)
    entering = lax.all_to_all(entering, "seq", split_axis=0, concat_axis=0, tiled=True)
    entering = entering.reshape(inner, state_width)

    scores = jnp.dot(c_rows, b_rows.T, preferred_element_type=F32)
    spread = running[:, None, :] - running[None, :, :]
    fall = jnp.exp(jnp.where(causal[:, :, None], spread, -jnp.inf))
    mixing = (scores[:, :, None] * fall * step_sizes[None, :, :]).astype(BF16)
    intra = jnp.einsum("tsh,shp->thp", mixing, inputs, preferred_element_type=F32)
    intra = intra.reshape(tokens, inner)
    own_head = (jnp.arange(inner)[None, :] // head_width == jnp.arange(heads)[:, None]).astype(F32)
    growth = jnp.dot(jnp.exp(running), own_head, precision=HIGHEST)
    arriving = growth * lax.dot_general(
        c_rows, entering, (((1,), (1,)), ((), ())), preferred_element_type=F32
    )
    ssm_out = intra + arriving + jnp.repeat(skip_gain, head_width)[None, :] * ssm_input.astype(F32)
    gated = ssm_out * jax.nn.silu(gate_input.astype(F32))
    normed = (
        gated
        * lax.rsqrt(jnp.mean(gated * gated, axis=1, keepdims=True) + 1e-05)
        * norm_gain[None, :]
    ).astype(BF16)

    def project(rows):
        parts = [
            jnp.dot(rows, w_group[k], preferred_element_type=F32).astype(BF16) for k in range(LOW)
        ]
        return jnp.concatenate(parts, axis=1)

    position = lax.axis_index("seq")
    mine = position // LOW
    come = [
        lax.ppermute(normed, "seq", [(i, (i + s * LOW) % n) for i in range(n)])
        for s in range(1, high)
    ]
    own = project(normed)
    gone = [
        lax.ppermute(project(come[s - 1]), "seq", [(i, (i - s * LOW) % n) for i in range(n)])
        for s in range(1, high)
    ]
    around = jnp.stack([own] + gone)
    mixer_out = jnp.concatenate(
        [
            lax.dynamic_index_in_dim(around, lax.rem(g - mine + high, high), 0, keepdims=False)
            for g in range(high)
        ],
        axis=1,
    )

    hidden = (residual.astype(F32) + mixer_out.astype(F32)).astype(BF16)
    hidden_wide = hidden.astype(F32)
    moe_input = (
        hidden_wide
        * lax.rsqrt(jnp.mean(hidden_wide * hidden_wide, axis=1, keepdims=True) + 1e-05)
        * moe_gain[None, :]
    ).astype(BF16)
    logits = jnp.dot(moe_input, router, preferred_element_type=F32)
    fanout = expert_ids.shape[1]
    capacity = tokens * fanout * 3 // (2 * n)
    picks = [
        (expert_ids[:, k : k + 1] == jnp.arange(n, dtype=jnp.int32)[None, :]).astype(F32)
        for k in range(fanout)
    ]
    earlier = (at[:, None] > at[None, :]).astype(BF16)
    before = jnp.dot(earlier, sum(picks).astype(BF16), preferred_element_type=F32)
    targets = [
        expert_ids[:, k] * capacity + jnp.sum(before * picks[k], axis=1).astype(jnp.int32)
        for k in range(fanout)
    ]
    powers = [jnp.exp(jnp.sum(logits * pick, axis=1)) for pick in picks]
    whole = sum(powers)
    slots = jnp.arange(n * capacity, dtype=jnp.int32)
    chosen = sum((slots[:, None] == target[None, :]).astype(F32) for target in targets)
    width = moe_input.shape[1]
    batch = jnp.dot(chosen.astype(BF16), moe_input, preferred_element_type=F32).astype(BF16)
    batch = lax.all_to_all(batch, "seq", split_axis=0, concat_axis=0, tiled=True)
    gate_part = jnp.dot(batch, w_gate[0], preferred_element_type=F32)
    up_part = jnp.dot(batch, w_up[0], preferred_element_type=F32)
    expert_hidden = (jax.nn.silu(gate_part) * up_part).astype(BF16)
    result = jnp.dot(expert_hidden, w_down[0], preferred_element_type=F32).astype(BF16)
    returned = lax.all_to_all(result, "seq", split_axis=0, concat_axis=0, tiled=True)
    weights = sum(
        jnp.where(target[:, None] == slots[None, :], (power / whole)[:, None], 0.0)
        for target, power in zip(targets, powers)
    )
    upper = lax.reduce_precision(weights, 8, 7)
    both = jnp.concatenate([upper.astype(BF16), (weights - upper).astype(BF16)], axis=0)
    mixed = jnp.dot(both, returned, preferred_element_type=F32)
    return (hidden_wide + mixed[:tokens] + mixed[tokens:]).astype(BF16)


def solution(mesh):
    rows = P(("batch", "seq"), None)
    experts = P("seq", None, None)
    in_specs = (
        rows,
        rows,
        rows,
        rows,
        rows,
        P(),
        P(),
        P(),
        P(),
        P(None, "seq"),
        rows,
        P(),
        P(),
        rows,
        experts,
        experts,
        experts,
    )
    return jax.shard_map(shards, mesh=mesh, in_specs=in_specs, out_specs=rows, check_vma=False)
```
